32 devices in a mesh: band: 4 (over y, core), tile: 8 (over z, x).
Axes of the slice: x: 2, y: 2, z: 4, core: 2. Of those that a mesh axis runs over, the one named last changes fastest.
Arguments:
- ocean_state: float32 [6, 64, 64, 1024], P(None, None, 'band', 'tile'), may hold values from -6 to 6
- forcing: float32 [6, 64, 64, 1024], P(None, None, 'band', 'tile')
- diffusivity: float32 [64, 1024], P('band', 'tile'), may hold values from 0.05 to 0.4
- land_sea: int32 [64, 1024], P('band', 'tile'), may hold values 0 or 1
- aggregate: int32 [64, 1024], P('band', 'tile'), may hold values from 0 to 63, as said below
- mixing: float32 [6, 6], replicated, may hold values from -2.5 to 2.5
- null_fields: float32 [2, 64, 2048], P(None, None, ('band', 'tile'))
- coarse_op: float32 [2048, 256], P('tile'), as said below
Outputs:
- new_state: float32 [6, 64, 64, 1024], P(None, None, 'band', 'tile')
- residual: float32 [6, 64, 64, 1024], P(None, None, 'band', 'tile')
The draws below stay inside these ranges and needn't reach their ends.
Inputs may be any that keep to these rules, and one draw needn't show every extreme that they name: `aggregate`: each coarse block of a device takes exactly 32 of that device's cells. `coarse_op`: each block of 256 rows has a positive diagonal.
All inputs are finite; a program needn't handle non-finite values. No bound on the sum of `land_sea` on one device may be relied on, other than what follows from the above.
Results may differ from the reference program's by a relative error of at most 0.0001.
Values sent between devices are 32-bit elements; how exact they have to be, the bound alone decides.
A program may use at most 192 MiB of HBM per device.

```python
import math
import jax
import jax.numpy as jnp
from jax import lax

FIELDS = 6
NZ = 64
CY = 16
CX = 128
CB = 64
SWEEPS = 3
NY = 64
NX = 1024
NCOL = 256
NCOARSE = 2048
N_BAND = 4
N_TILE = 8


def draw_forcing(key, part):
    key = jax.random.fold_in(key, 11)
    key_rough, key_shift = jax.random.split(key)
    rough = jax.random.normal(key_rough, (FIELDS, NZ, NY, NX), jnp.float32)
    shift = jax.random.uniform(key_shift, (FIELDS, NZ, 1, 1), jnp.float32, -2.0, 2.0)
    return rough + shift


def draw_aggregate(key, part):
    key = jax.random.fold_in(key, 23)
    cells = CY * CX
    pattern = jnp.arange(cells, dtype=jnp.int32) % CB
    key_list = jax.random.split(key, N_BAND * N_TILE)
    shuffled = jax.vmap(lambda sub_key: jax.random.permutation(sub_key, pattern))(key_list)
    blocks = shuffled.reshape(N_BAND, N_TILE, CY, CX).transpose(0, 2, 1, 3)
    return blocks.reshape(NY, NX).astype(jnp.int32)


def draw_null_fields(key, part):
    key = jax.random.fold_in(key, 37)
    key_first, key_second = jax.random.split(key)
    first_vec = jax.random.uniform(key_first, (1, NZ, NCOARSE), jnp.float32, 0.5, 1.5)
    second_vec = jax.random.normal(key_second, (1, NZ, NCOARSE), jnp.float32)
    return jnp.concatenate([first_vec, second_vec], axis=0)


def draw_coarse_op(key, part):
    key = jax.random.fold_in(key, 41)
    key_off, key_diag = jax.random.split(key)
    shape_all = (N_TILE * NCOL, NCOL)
    scale_off = 0.5 / jnp.sqrt(jnp.float32(NCOL))
    off_part = jax.random.normal(key_off, shape_all, jnp.float32) * scale_off
    diag_part = jax.random.uniform(key_diag, shape_all, jnp.float32, 3.0, 5.0)
    row_index = jnp.arange(N_TILE * NCOL, dtype=jnp.int32)[:, None] % NCOL
    col_index = jnp.arange(NCOL, dtype=jnp.int32)[None, :]
    return jnp.where(row_index == col_index, diag_part, off_part)


def plant(drawn, stream_key, low, high):
    longest = drawn.shape.index(max(drawn.shape))
    spots = []
    for shift in (0, 1):
        where = [jax.random.randint(jax.random.fold_in(stream_key, axis), (), 0, length) for axis, length in enumerate(drawn.shape)]
        where[longest] = (where[longest] + shift) % drawn.shape[longest]
        spots.append(tuple(where))
    return drawn.at[spots[0]].set(low).at[spots[1]].set(high)


def block_levels(stream_key, dims, pieces, smallest, largest):
    factor_of = 1.0
    for dim, shards_of in pieces:
        draws = jax.random.uniform(jax.random.fold_in(jax.random.fold_in(stream_key, 6), dim), (shards_of,), jnp.float32, smallest / len(pieces), largest / len(pieces))
        factor_of = factor_of * jnp.repeat(jnp.exp(draws), dims[dim] // shards_of).reshape((-1,) + (1,) * (len(dims) - 1 - dim))
    return factor_of


def gaussian(own_key, extent, spread, most, cuts=(), kind=jnp.bfloat16):
    values = jax.random.normal(own_key, extent, jnp.float32) * spread
    if len(cuts) > 0:
        values = block_levels(own_key, extent, cuts, -0.22, 0.18) * values
    return jnp.clip(values, min=-most, max=most).astype(kind)


def setup_inputs(seed: int = 0) -> dict:
    keys = jax.random.split(jax.random.key(seed), 9)
    ocean_state = gaussian(keys[0], (FIELDS, NZ, NY, NX), 1.0, 6.0, ((2, 4), (3, 8)), jnp.float32)
    forcing = draw_forcing(jax.random.fold_in(keys[8], 71), 0)
    diffusivity = jnp.clip(jnp.exp(math.log(0.4) - 2.0794415 * jax.random.uniform(keys[2], (NY, NX), jnp.float32) ** block_levels(keys[2], (NY, NX), ((0, 4), (1, 8)), -0.2, 0.2)), 0.05, 0.4)
    land_sea = plant((jax.random.randint(keys[3], (NY, NX), 0, 4) < 3).astype(jnp.int32), jax.random.fold_in(keys[3], 1), 0, 1)
    aggregate = draw_aggregate(jax.random.fold_in(keys[8], 71), 0)
    mixing = gaussian(keys[5], (FIELDS, FIELDS), FIELDS ** -0.5, 2.5, (), jnp.float32)
    null_fields = draw_null_fields(jax.random.fold_in(keys[8], 71), 0)
    coarse_op = draw_coarse_op(jax.random.fold_in(keys[8], 71), 0)
    return dict(ocean_state=ocean_state, forcing=forcing, diffusivity=diffusivity, land_sea=land_sea, aggregate=aggregate, mixing=mixing, null_fields=null_fields, coarse_op=coarse_op)


SPEED_TABLE = (0.3, -0.2, 0.1, 0.25, -0.15, 0.05)
VERTICAL_MIX = 0.3
TIME_WEIGHT = 0.5
RESTRICT_SCALE = 0.25


def jacobian(field, diffusivity, ocean_mask, mixing):
    padded = jnp.pad(field, ((0, 0), (0, 0), (1, 1), (1, 1)))
    center = padded[:, :, 1:-1, 1:-1]
    laplace_h = padded[:, :, 2:, 1:-1] + padded[:, :, :-2, 1:-1] + padded[:, :, 1:-1, 2:] + padded[:, :, 1:-1, :-2] - 4.0 * center
    zonal_diff = padded[:, :, 1:-1, 2:] - padded[:, :, 1:-1, :-2]
    column_pad = jnp.pad(center, ((0, 0), (1, 1), (0, 0), (0, 0)))
    laplace_z = column_pad[:, 2:] + column_pad[:, :-2] - 2.0 * center
    coupled = jnp.einsum("fg,gzyx->fzyx", mixing, center, precision=lax.Precision.HIGHEST)
    speeds = jnp.array(SPEED_TABLE, dtype=jnp.float32)[:, None, None, None]
    inner = center - diffusivity * laplace_h - VERTICAL_MIX * laplace_z + speeds * zonal_diff + coupled
    return ocean_mask * inner + (1.0 - ocean_mask) * center


def reference(ocean_state, forcing, diffusivity, land_sea, aggregate, mixing, null_fields, coarse_op):
    ocean_mask = land_sea.astype(jnp.float32)
    first_jvp = jacobian(ocean_state, diffusivity, ocean_mask, mixing)
    second_jvp = jacobian(first_jvp, diffusivity, ocean_mask, mixing)
    residual = forcing - (first_jvp + TIME_WEIGHT * second_jvp)
    lat_index = jnp.arange(NY, dtype=jnp.int32)[:, None] // CY
    lon_index = jnp.arange(NX, dtype=jnp.int32)[None, :] // CX
    global_block = ((lat_index * N_TILE + lon_index) * CB + aggregate).reshape(-1).astype(jnp.int32)
    flat_rows = residual.reshape(FIELDS * NZ, NY * NX)
    coarse = jax.ops.segment_sum(flat_rows.T, global_block, num_segments=NCOARSE).T
    coarse = RESTRICT_SCALE * coarse.reshape(FIELDS, NZ, N_BAND, N_TILE * CB)
    null_pair = null_fields.reshape(2, NZ, N_BAND, N_TILE * CB)
    gram = jnp.einsum("kzbc,lzbc->klzb", null_pair, null_pair, precision=lax.Precision.HIGHEST)
    proj = jnp.einsum("kzbc,fzbc->kfzb", null_pair, coarse, precision=lax.Precision.HIGHEST)
    determinant = gram[0, 0] * gram[1, 1] - gram[0, 1] * gram[0, 1]
    coef_first = (gram[1, 1] * proj[0] - gram[0, 1] * proj[1]) / determinant
    coef_second = (gram[0, 0] * proj[1] - gram[0, 1] * proj[0]) / determinant
    deflated = coarse - coef_first[..., None] * null_pair[0][None] - coef_second[..., None] * null_pair[1][None]
    columns = deflated.reshape(FIELDS, NZ, N_BAND, N_TILE, CB).transpose(3, 0, 1, 2, 4).reshape(N_TILE, FIELDS * NZ, NCOL)
    operators = coarse_op.reshape(N_TILE, NCOL, NCOL)
    diagonal_vals = jnp.diagonal(operators, axis1=1, axis2=2)[:, None, :]
    iterate = jnp.zeros_like(columns)
    for sweep_index in range(SWEEPS):
        applied = jnp.einsum("trc,tjc->trj", iterate, operators, precision=lax.Precision.HIGHEST)
        iterate = iterate + (columns - applied) / diagonal_vals
    smoothed = iterate.reshape(N_TILE, FIELDS, NZ, N_BAND, CB).transpose(1, 2, 3, 0, 4).reshape(FIELDS * NZ, NCOARSE)
    correction = jnp.take(smoothed, global_block, axis=1).reshape(FIELDS, NZ, NY, NX)
    return ocean_state + correction, residual
```

```python
import functools

import jax
import jax.numpy as jnp
from jax import lax
from jax.experimental import pallas as pl
from jax.experimental.pallas import tpu as pltpu
from jax.sharding import PartitionSpec as P

SWEEPS = 3
SPEED_TABLE = (0.3, -0.2, 0.1, 0.25, -0.15, 0.05)
VERTICAL_MIX = 0.3
TIME_WEIGHT = 0.5
RESTRICT_SCALE = 0.25

F32 = jnp.float32
BF16 = jnp.bfloat16
MESH = pl.DeviceIdType.MESH
PAD = 8
ZC = 16
MIB = 1 << 20


def nt_dot(a, b, precision=None):
    return lax.dot_general(
        a, b, (((1,), (1,)), ((), ())), precision=precision, preferred_element_type=F32
    )


def main_kernel(
    dims, ocean_ref, forcing_ref, diff_ref, land_ref, agg_ref, mix_ref, null_ref, op_ref,
    res_ref, smooth_ref,
    ocean, work, field0, field1, send_w, send_e, col_w, col_e, hi, lo, coarse,
    mom, slab_out, slab_in, back_out, back_in,
    in_sem, work_sem, out_sem, lat_send, lat_recv, lon_send, lon_recv,
    mom_send, mom_recv, slab_send, slab_recv, back_send, back_recv,
):
    n_band, n_tile, nf, nz, cy, cx, cb = dims
    band, tile = lax.axis_index("band"), lax.axis_index("tile")
    top = PAD + nz

    loads = [
        pltpu.make_async_copy(ocean_ref.at[f], ocean.at[f], in_sem.at[f]) for f in range(nf)
    ]
    for load in loads:
        load.start()
    load_forcing = pltpu.make_async_copy(forcing_ref, work, work_sem)
    load_forcing.start()

    barrier = pltpu.get_barrier_semaphore()
    for d in range(1, n_tile):
        pl.semaphore_signal(
            barrier, inc=1, device_id=(band, lax.rem(tile + d, n_tile)), device_id_type=MESH
        )
    for d in range(1, n_band):
        pl.semaphore_signal(
            barrier, inc=1, device_id=(lax.rem(band + d, n_band), tile), device_id_type=MESH
        )

    zpad = jnp.zeros((nf, cy + 2, PAD, cx), F32)
    for field in (field0, field1):
        field[:, :, 0:PAD, :] = zpad
        field[:, :, top : top + PAD, :] = zpad
    zrow = jnp.zeros((nf, nz, cx), F32)

    @pl.when(band == 0)
    def _():
        for field in (field0, field1):
            field[:, 0, PAD:top, :] = zrow

    @pl.when(band == n_band - 1)
    def _():
        for field in (field0, field1):
            field[:, cy + 1, PAD:top, :] = zrow

    zcol = jnp.zeros((2, nz, cx), F32)

    @pl.when(tile == 0)
    def _():
        col_w[...] = zcol

    @pl.when(tile == n_tile - 1)
    def _():
        col_e[...] = zcol

    send_w[...] = zcol
    send_e[...] = zcol
    coarse[...] = jnp.zeros_like(coarse)

    lane = lax.broadcasted_iota(jnp.int32, (ZC, cx), 1)

    def pack(which, value, rows, k):
        here = lane == k
        send_w[which, rows, :] = jnp.where(here, pltpu.roll(value, k, 1), send_w[which, rows, :])
        shift = lax.rem(k + 1, cx)
        send_e[which, rows, :] = jnp.where(
            here, pltpu.roll(value, shift, 1), send_e[which, rows, :]
        )

    for f in range(nf):
        loads[f].wait()

    def fill(y, carry):
        for f in range(nf):
            for z0 in range(0, nz, ZC):
                value = ocean[f, pl.ds(z0 * cy + y, ZC, stride=cy), :]
                field0[f, y + 1, PAD + z0 : PAD + z0 + ZC, :] = value
                pack(0, value, slice(z0, z0 + ZC), f * cy + y)
        return carry

    lax.fori_loop(0, cy, fill, 0)
    pl.semaphore_wait(barrier, n_tile + n_band - 2)

    def lat_copies(which, field):
        up = pltpu.make_async_remote_copy(
            src_ref=field.at[:, cy, PAD:top, :], dst_ref=field.at[:, 0, PAD:top, :],
            send_sem=lat_send.at[which, 0], recv_sem=lat_recv.at[which, 0],
            device_id=(band + 1, tile), device_id_type=MESH,
        )
        down = pltpu.make_async_remote_copy(
            src_ref=field.at[:, 1, PAD:top, :], dst_ref=field.at[:, cy + 1, PAD:top, :],
            send_sem=lat_send.at[which, 1], recv_sem=lat_recv.at[which, 1],
            device_id=(band - 1, tile), device_id_type=MESH,
        )
        return up, down

    def lon_copies(which):
        up = pltpu.make_async_remote_copy(
            src_ref=send_e.at[which], dst_ref=col_w.at[which],
            send_sem=lon_send.at[which, 0], recv_sem=lon_recv.at[which, 0],
            device_id=(band, tile + 1), device_id_type=MESH,
        )
        down = pltpu.make_async_remote_copy(
            src_ref=send_w.at[which], dst_ref=col_e.at[which],
            send_sem=lon_send.at[which, 1], recv_sem=lon_recv.at[which, 1],
            device_id=(band, tile - 1), device_id_type=MESH,
        )
        return up, down

    def start_both(copies, index, count):
        @pl.when(index < count - 1)
        def _():
            copies[0].start()

        @pl.when(index > 0)
        def _():
            copies[1].start()

    def recv_both(copies, index, count):
        @pl.when(index > 0)
        def _():
            copies[0].wait_recv()

        @pl.when(index < count - 1)
        def _():
            copies[1].wait_recv()

    def sent_both(copies, index, count):
        @pl.when(index < count - 1)
        def _():
            copies[0].wait_send()

        @pl.when(index > 0)
        def _():
            copies[1].wait_send()

    def exchange(which, field):
        lon, lat = lon_copies(which), lat_copies(which, field)
        start_both(lon, tile, n_tile)
        start_both(lat, band, n_band)
        return lon, lat

    def jacobian_rows(which, field, y, z0):
        at = PAD + z0
        rows = slice(at, at + ZC)
        center = [field[g, y + 1, rows, :] for g in range(nf)]
        diff = diff_ref[pl.ds(y, 1), :]
        main = 4.0 * diff + (1.0 + 2.0 * VERTICAL_MIX)
        ocean_cell = jnp.broadcast_to(land_ref[pl.ds(y, 1), :], (ZC, cx)) != 0
        west_in = col_w[which, z0 : z0 + ZC, :]
        east_in = col_e[which, z0 : z0 + ZC, :]
        outs = []
        for f in range(nf):
            c = center[f]
            k = f * cy + y
            west = jnp.where(lane == 0, pltpu.roll(west_in, cx - k, 1), pltpu.roll(c, 1, 1))
            east = jnp.where(
                lane == cx - 1, pltpu.roll(east_in, cx - 1 - k, 1), pltpu.roll(c, cx - 1, 1)
            )
            around = field[f, y, rows, :] + field[f, y + 2, rows, :] + (east + west)
            vert = field[f, y + 1, at - 1 : at - 1 + ZC, :] + field[f, y + 1, at + 1 : at + 1 + ZC, :]
            total = main * c - diff * around - VERTICAL_MIX * vert + SPEED_TABLE[f] * (east - west)
            for g in range(nf):
                total = total + mix_ref[f, g] * center[g]
            outs.append(jnp.where(ocean_cell, total, c))
        return center, outs

    def first(y, carry):
        for z0 in range(0, nz, ZC):
            center, outs = jacobian_rows(0, field0, y, z0)
            for f in range(nf):
                field1[f, y + 1, PAD + z0 : PAD + z0 + ZC, :] = outs[f]
                pack(1, outs[f], slice(z0, z0 + ZC), f * cy + y)
        return carry

    def second(y, carry):
        for z0 in range(0, nz, ZC):
            center, outs = jacobian_rows(1, field1, y, z0)
            for f in range(nf):
                spot = pl.ds(z0 * cy + y, ZC, stride=cy)
                value = work[f, spot, :] - (center[f] + TIME_WEIGHT * outs[f])
                work[f, spot, :] = value
                high = value.astype(BF16)
                hi[f * nz + z0 : f * nz + z0 + ZC, :] = high
                lo[f * nz + z0 : f * nz + z0 + ZC, :] = (value - high.astype(F32)).astype(BF16)
        block = lax.broadcasted_iota(jnp.int32, (cx, cx), 0)
        member = jnp.where(block == agg_ref[pl.ds(y, 1), :], 1.0, 0.0).astype(BF16)
        coarse[...] += nt_dot(hi[...], member) + nt_dot(lo[...], member)
        return carry

    ends = lambda body: lax.fori_loop(0, 2, lambda i, carry: body(i * (cy - 1), carry), 0)

    lon0, lat0 = exchange(0, field0)
    recv_both(lon0, tile, n_tile)
    lax.fori_loop(1, cy - 1, first, 0)
    recv_both(lat0, band, n_band)
    ends(first)
    lon1, lat1 = exchange(1, field1)
    load_forcing.wait()
    recv_both(lon1, tile, n_tile)
    lax.fori_loop(1, cy - 1, second, 0)
    recv_both(lat1, band, n_band)
    ends(second)
    store = pltpu.make_async_copy(work, res_ref, out_sem)
    store.start()

    nulls = [null_ref[0], null_ref[1]]
    parts = [RESTRICT_SCALE * coarse[f * nz : (f + 1) * nz, 0:cb] for f in range(nf)]
    products = [nulls[0] * nulls[0], nulls[0] * nulls[1], nulls[1] * nulls[1]]
    for k in range(2):
        products += [nulls[k] * part for part in parts]
    wide = lax.broadcasted_iota(jnp.int32, (nz, cx), 1)
    table = jnp.zeros((nz, cx), F32)
    for j, product in enumerate(products):
        table = jnp.where(wide == j, jnp.sum(product, axis=1, keepdims=True), table)
    square = jnp.concatenate([table, jnp.zeros((cx - nz, cx), F32)], axis=0)
    mom[tile] = jnp.transpose(square)[0:16, :]

    def mom_copy(partner, slot):
        return pltpu.make_async_remote_copy(
            src_ref=mom.at[tile], dst_ref=mom.at[slot],
            send_sem=mom_send.at[partner], recv_sem=mom_recv.at[slot],
            device_id=(band, partner), device_id_type=MESH,
        )

    for d in range(1, n_tile):
        mom_copy(lax.rem(tile + d, n_tile), tile).start()

    op = op_ref[...]
    ncol = op.shape[0]
    same = lax.broadcasted_iota(jnp.int32, (ncol, ncol), 0) == lax.broadcasted_iota(
        jnp.int32, (ncol, ncol), 1
    )
    diagonal = jnp.sum(jnp.where(same, op, 0.0), axis=0, keepdims=True)

    for d in range(1, n_tile):
        other = lax.rem(tile + d, n_tile)
        mom_copy(other, other).wait_recv()
    total = mom[0]
    for t in range(1, n_tile):
        total = total + mom[t]
    row = lambda j: total[j : j + 1, :]
    g00, g01, g11 = row(0), row(1), row(2)
    p0, p1 = total[3 : 3 + nf, :], total[3 + nf : 3 + 2 * nf, :]
    real = lax.broadcasted_iota(jnp.int32, (1, cx), 1) < nz
    det = jnp.where(real, g00 * g11 - g01 * g01, 1.0)
    c0 = (g11 * p0 - g01 * p1) / det
    c1 = (g00 * p1 - g01 * p0) / det
    coefs = jnp.concatenate([c0, c1, jnp.zeros((cx - 2 * nf, cx), F32)], axis=0)
    coefs = jnp.transpose(coefs)[0:nz, :]
    half = nf // 2
    deflated = [
        parts[f] - coefs[:, f : f + 1] * nulls[0] - coefs[:, nf + f : nf + f + 1] * nulls[1]
        for f in range(nf)
    ]
    slab = nz // n_band
    for f in range(half):
        both = jnp.concatenate([deflated[f], deflated[f + half]], axis=1)
        for d in range(n_band):
            slab_out[d, f * slab : (f + 1) * slab, :] = both[d * slab : (d + 1) * slab, :]

    def band_copy(out, into, sends, recvs, partner, slot):
        return pltpu.make_async_remote_copy(
            src_ref=out.at[partner], dst_ref=into.at[slot],
            send_sem=sends.at[partner], recv_sem=recvs.at[slot],
            device_id=(partner, tile), device_id_type=MESH,
        )

    def swap(out, into, sends, recvs):
        for d in range(1, n_band):
            band_copy(out, into, sends, recvs, lax.rem(band + d, n_band), band).start()
        into[band] = out[band]
        for d in range(1, n_band):
            other = lax.rem(band + d, n_band)
            band_copy(out, into, sends, recvs, other, other).wait_recv()

    swap(slab_out, slab_in, slab_send, slab_recv)
    pieces = [slab_in[b] for b in range(n_band)]
    lows = jnp.concatenate([piece[:, 0:cb] for piece in pieces], axis=1)
    highs = jnp.concatenate([piece[:, cb : 2 * cb] for piece in pieces], axis=1)
    columns = jnp.concatenate([lows, highs], axis=0)
    iterate = columns / diagonal
    for _ in range(SWEEPS - 1):
        applied = nt_dot(iterate, op, lax.Precision.HIGHEST)
        iterate = iterate + (columns - applied) / diagonal
    rows_half = half * slab
    for b in range(n_band):
        mine = slice(b * cb, (b + 1) * cb)
        back_out[b] = jnp.concatenate(
            [iterate[0:rows_half, mine], iterate[rows_half : 2 * rows_half, mine]], axis=1
        )
    swap(back_out, back_in, back_send, back_recv)
    inside = lax.broadcasted_iota(jnp.int32, (slab, 2 * cb), 1) < cb
    for d in range(n_band):
        for f in range(half):
            both = back_in[d, f * slab : (f + 1) * slab, :]
            z = slice(d * slab, (d + 1) * slab)
            smooth_ref[f, z, :] = jnp.where(inside, both, 0.0)
            smooth_ref[f + half, z, :] = jnp.where(inside, pltpu.roll(both, cb, 1), 0.0)

    for lon, lat in ((lon0, lat0), (lon1, lat1)):
        sent_both(lon, tile, n_tile)
        sent_both(lat, band, n_band)
    for d in range(1, n_tile):
        mom_copy(lax.rem(tile + d, n_tile), tile).wait_send()
    for d in range(1, n_band):
        other = lax.rem(band + d, n_band)
        band_copy(slab_out, slab_in, slab_send, slab_recv, other, band).wait_send()
        band_copy(back_out, back_in, back_send, back_recv, other, band).wait_send()
    store.wait()


def finish_kernel(cy, ocean_ref, res_ref, smooth_ref, agg_ref, new_ref, out_ref):
    nz, cx = smooth_ref.shape[1:]
    value = smooth_ref[0]
    high = value.astype(BF16)
    low = (value - high.astype(F32)).astype(BF16)
    block = lax.broadcasted_iota(jnp.int32, (cx, cx), 0)
    for y in range(cy):
        member = jnp.where(block == agg_ref[y : y + 1, :], 1.0, 0.0).astype(BF16)
        add = jnp.dot(high, member, preferred_element_type=F32) + jnp.dot(
            low, member, preferred_element_type=F32
        )
        spot = pl.ds(y, nz, stride=cy)
        new_ref[0, spot, :] = ocean_ref[0, spot, :] + add
    out_ref[...] = res_ref[...]


def shards(
    n_band, n_tile, ocean_state, forcing, diffusivity, land_sea, aggregate, mixing, null_fields,
    coarse_op,
):
    nf, nz, cy, cx = ocean_state.shape
    cb = null_fields.shape[2]
    slab = nz // n_band
    ocean_rows = ocean_state.reshape(nf, nz * cy, cx)
    forcing_rows = forcing.reshape(nf, nz * cy, cx)
    dims = (n_band, n_tile, nf, nz, cy, cx, cb)
    any_spec = pl.BlockSpec(memory_space=pl.ANY)
    vmem = pl.BlockSpec(memory_space=pltpu.VMEM)
    smem = pl.BlockSpec(memory_space=pltpu.SMEM)
    field = pltpu.VMEM((nf, cy + 2, nz + 2 * PAD, cx), F32)
    strip = pltpu.VMEM((2, nz, cx), F32)
    slabs = pltpu.VMEM((n_band, nf // 2 * slab, 2 * cb), F32)
    dma = pltpu.SemaphoreType.DMA
    cells = nf * nz * cy * cx
    residual, smoothed = pl.pallas_call(
        functools.partial(main_kernel, dims),
        out_shape=(
            jax.ShapeDtypeStruct((nf, nz * cy, cx), F32),
            jax.ShapeDtypeStruct((nf, nz, 2 * cb), F32),
        ),
        in_specs=[any_spec, any_spec, vmem, vmem, vmem, smem, vmem, vmem],
        out_specs=(any_spec, vmem),
        scratch_shapes=[
            pltpu.VMEM((nf, nz * cy, cx), F32),
            pltpu.VMEM((nf, nz * cy, cx), F32),
            field, field, strip, strip, strip, strip,
            pltpu.VMEM((nf * nz, cx), BF16),
            pltpu.VMEM((nf * nz, cx), BF16),
            pltpu.VMEM((nf * nz, cx), F32),
            pltpu.VMEM((n_tile, 16, cx), F32),
            slabs, slabs, slabs, slabs,
            dma((nf,)), dma, dma,
            dma((2, 2)), dma((2, 2)), dma((2, 2)), dma((2, 2)),
            dma((n_tile,)), dma((n_tile,)),
            dma((n_band,)), dma((n_band,)), dma((n_band,)), dma((n_band,)),
        ],
        compiler_params=pltpu.CompilerParams(
            collective_id=0, has_side_effects=True, vmem_limit_bytes=40 * MIB
        ),
        cost_estimate=pl.CostEstimate(
            flops=60 * cells, bytes_accessed=12 * cells, transcendentals=0
        ),
    )(ocean_rows, forcing_rows, diffusivity, land_sea, aggregate, mixing, null_fields, coarse_op)

    rows_spec = pl.BlockSpec((1, nz * cy, cx), lambda f: (f, 0, 0))
    new_state, residual = pl.pallas_call(
        functools.partial(finish_kernel, cy),
        grid=(nf,),
        out_shape=(
            jax.ShapeDtypeStruct((nf, nz * cy, cx), F32),
            jax.ShapeDtypeStruct((nf, nz * cy, cx), F32),
        ),
        in_specs=[
            rows_spec, rows_spec,
            pl.BlockSpec((1, nz, 2 * cb), lambda f: (f, 0, 0)),
            pl.BlockSpec((cy, cx), lambda f: (0, 0)),
        ],
        out_specs=(rows_spec, rows_spec),
        compiler_params=pltpu.CompilerParams(vmem_limit_bytes=24 * MIB),
        cost_estimate=pl.CostEstimate(
            flops=4 * cells, bytes_accessed=16 * cells, transcendentals=0
        ),
    )(ocean_rows, residual, smoothed, aggregate)
    shape = ocean_state.shape
    return (new_state.reshape(shape), residual.reshape(shape))


def solution(mesh):
    sizes = dict(mesh.shape)
    return jax.shard_map(
        functools.partial(shards, sizes["band"], sizes["tile"]),
        mesh=mesh,
        in_specs=(
            P(None, None, "band", "tile"),
            P(None, None, "band", "tile"),
            P("band", "tile"),
            P("band", "tile"),
            P("band", "tile"),
            P(),
            P(None, None, ("band", "tile")),
            P("tile", None),
        ),
        out_specs=(P(None, None, "band", "tile"), P(None, None, "band", "tile")),
        check_vma=False,
    )
```

```python
import functools

import jax
import jax.numpy as jnp
from jax import lax
from jax.experimental import pallas as pl
from jax.experimental.pallas import tpu as pltpu
from jax.sharding import PartitionSpec as P

SWEEPS = 3
SPEED_TABLE = (0.3, -0.2, 0.1, 0.25, -0.15, 0.05)
VERTICAL_MIX = 0.3
TIME_WEIGHT = 0.5
RESTRICT_SCALE = 0.25

F32 = jnp.float32
BF16 = jnp.bfloat16
MESH = pl.DeviceIdType.MESH
PAD = 8
ZC = 64
MIB = 1 << 20


def nt_dot(a, b, precision=None):
    return lax.dot_general(
        a, b, (((1,), (1,)), ((), ())), precision=precision, preferred_element_type=F32
    )


def main_kernel(
    dims, ocean_ref, forcing_ref, diff_hbm, land_hbm, agg_hbm, mix_hbm, null_hbm, op_hbm,
    res_ref, smooth_ref,
    diff_ref, land_ref, agg_ref, mix_ref, null_ref, op_ref, small_sem,
    ocean, work, field0, field1, edges, halo, col_w, col_e, hi, lo, coarse,
    mom, slab_out, slab_in, back_out, back_in,
    in_sem, work_sem, out_sem, lat_send, lat_recv, lon_send, lon_recv,
    mom_send, mom_recv, slab_send, slab_recv, back_send, back_recv,
):
    n_band, n_tile, nf, nz, cy, cx, cb = dims
    band, tile = lax.axis_index("band"), lax.axis_index("tile")
    top = PAD + nz

    loads = [
        pltpu.make_async_copy(ocean_ref.at[f], ocean.at[f], in_sem.at[f]) for f in range(nf)
    ]
    for load in loads:
        load.start()
    smalls = [
        pltpu.make_async_copy(source, target, small_sem.at[i])
        for i, (source, target) in enumerate(
            (
                (diff_hbm, diff_ref), (land_hbm, land_ref), (agg_hbm, agg_ref),
                (mix_hbm, mix_ref), (null_hbm, null_ref), (op_hbm, op_ref),
            )
        )
    ]
    for load in smalls:
        load.start()
    load_forcing = pltpu.make_async_copy(forcing_ref, work, work_sem)
    load_forcing.start()

    barrier = pltpu.get_barrier_semaphore()
    for d in range(1, n_tile):
        pl.semaphore_signal(
            barrier, inc=1, device_id=(band, lax.rem(tile + d, n_tile)), device_id_type=MESH
        )
    for d in range(1, n_band):
        pl.semaphore_signal(
            barrier, inc=1, device_id=(lax.rem(band + d, n_band), tile), device_id_type=MESH
        )

    zpad = jnp.zeros((nf, cy + 2, PAD, cx), F32)
    for field in (field0, field1):
        field[:, :, 0:PAD, :] = zpad
        field[:, :, top : top + PAD, :] = zpad
    zrow = jnp.zeros((nf, nz, cx), F32)

    @pl.when(band == 0)
    def _():
        for field in (field0, field1):
            field[:, 0, PAD:top, :] = zrow

    @pl.when(band == n_band - 1)
    def _():
        for field in (field0, field1):
            field[:, cy + 1, PAD:top, :] = zrow

    zcol = jnp.zeros((2, 2, nz, cx), F32)

    @pl.when(tile == 0)
    def _():
        col_w[...] = zcol

    @pl.when(tile == n_tile - 1)
    def _():
        col_e[...] = zcol

    edges[...] = zcol
    coarse[...] = jnp.zeros_like(coarse)

    lane = lax.broadcasted_iota(jnp.int32, (ZC, cx), 1)

    pair = lane // 2
    group_rows = cy // 2

    def place(f, y):
        return f * group_rows + lax.rem(y + cy - 1, group_rows)

    def pack(carry, value, k):
        return jnp.where(pair == k, pltpu.roll(value, 2 * k + 1, 1), carry)

    def sweep(body, which, group, start, stop, stride=1):
        for z0 in range(0, nz, ZC):
            packed = lax.fori_loop(
                start, stop, lambda i, carry: body(z0, i * stride, carry), jnp.zeros((ZC, cx), F32)
            )
            rows = slice(z0, z0 + ZC)
            edges[which, group, rows, :] = edges[which, group, rows, :] + packed

    for f in range(nf):
        loads[f].wait()

    def fill(z0, y, carry):
        for f in range(nf):
            value = ocean[f, pl.ds(z0 * cy + y, ZC, stride=cy), :]
            field0[f, y + 1, PAD + z0 : PAD + z0 + ZC, :] = value
            carry = pack(carry, value, place(f, y))
        return carry

    def lat_copies(which, field):
        up = pltpu.make_async_remote_copy(
            src_ref=field.at[:, cy, PAD:top, :], dst_ref=field.at[:, 0, PAD:top, :],
            send_sem=lat_send.at[which, 0], recv_sem=lat_recv.at[which, 0],
            device_id=(band + 1, tile), device_id_type=MESH,
        )
        down = pltpu.make_async_remote_copy(
            src_ref=field.at[:, 1, PAD:top, :], dst_ref=field.at[:, cy + 1, PAD:top, :],
            send_sem=lat_send.at[which, 1], recv_sem=lat_recv.at[which, 1],
            device_id=(band - 1, tile), device_id_type=MESH,
        )
        return up, down

    def lon_copies(which, group):
        up = pltpu.make_async_remote_copy(
            src_ref=edges.at[which, group], dst_ref=col_w.at[which, group],
            send_sem=lon_send.at[which, group, 0], recv_sem=lon_recv.at[which, group, 0],
            device_id=(band, tile + 1), device_id_type=MESH,
        )
        down = pltpu.make_async_remote_copy(
            src_ref=edges.at[which, group], dst_ref=col_e.at[which, group],
            send_sem=lon_send.at[which, group, 1], recv_sem=lon_recv.at[which, group, 1],
            device_id=(band, tile - 1), device_id_type=MESH,
        )
        return up, down

    def start_both(copies, index, count):
        @pl.when(index < count - 1)
        def _():
            copies[0].start()

        @pl.when(index > 0)
        def _():
            copies[1].start()

    def recv_both(copies, index, count):
        @pl.when(index > 0)
        def _():
            copies[0].wait_recv()

        @pl.when(index < count - 1)
        def _():
            copies[1].wait_recv()

    even = lax.broadcasted_iota(jnp.int32, (nz, cx), 1) % 2 == 0

    def recv_lon(which, group):
        recv_both(lon[which][group], tile, n_tile)
        halo[which, group] = jnp.where(
            even, col_w[which, group], pltpu.roll(col_e[which, group], cx - 2, 1)
        )

    def sent_both(copies, index, count):
        @pl.when(index < count - 1)
        def _():
            copies[0].wait_send()

        @pl.when(index > 0)
        def _():
            copies[1].wait_send()

    def jacobian_rows(which, group, field, y, z0):
        at = PAD + z0
        rows = slice(at, at + ZC)
        center = [field[g, y + 1, rows, :] for g in range(nf)]
        diff = diff_ref[pl.ds(y, 1), :]
        main = 4.0 * diff + (1.0 + 2.0 * VERTICAL_MIX)
        ocean_cell = jnp.broadcast_to(land_ref[pl.ds(y, 1), :], (ZC, cx)) != 0
        beside = halo[which, group, z0 : z0 + ZC, :]
        outs = []
        for f in range(nf):
            c = center[f]
            k = place(f, y)
            outer = pltpu.roll(beside, lax.rem(cx - 2 * k, cx), 1)
            west = jnp.where(lane == 0, outer, pltpu.roll(c, 1, 1))
            east = jnp.where(lane == cx - 1, outer, pltpu.roll(c, cx - 1, 1))
            around = field[f, y, rows, :] + field[f, y + 2, rows, :] + (east + west)
            vert = field[f, y + 1, at - 1 : at - 1 + ZC, :] + field[f, y + 1, at + 1 : at + 1 + ZC, :]
            total = main * c - diff * around - VERTICAL_MIX * vert + SPEED_TABLE[f] * (east - west)
            for g in range(nf):
                total = total + mix_ref[f, g] * center[g]
            outs.append(jnp.where(ocean_cell, total, c))
        return center, outs

    def first(group):
        def body(z0, y, carry):
            center, outs = jacobian_rows(0, group, field0, y, z0)
            for f in range(nf):
                field1[f, y + 1, PAD + z0 : PAD + z0 + ZC, :] = outs[f]
                carry = pack(carry, outs[f], place(f, y))
            return carry

        return body

    def second(group, y, carry):
        for z0 in range(0, nz, ZC):
            center, outs = jacobian_rows(1, group, field1, y, z0)
            for f in range(nf):
                spot = pl.ds(z0 * cy + y, ZC, stride=cy)
                value = work[f, spot, :] - (center[f] + TIME_WEIGHT * outs[f])
                work[f, spot, :] = value
                high = value.astype(BF16)
                hi[f * nz + z0 : f * nz + z0 + ZC, :] = high
                lo[f * nz + z0 : f * nz + z0 + ZC, :] = (value - high.astype(F32)).astype(BF16)
        block = lax.broadcasted_iota(jnp.int32, (cx, cx), 0)
        member = jnp.where(block == agg_ref[pl.ds(y, 1), :], 1.0, 0.0).astype(BF16)
        coarse[...] += nt_dot(hi[...], member) + nt_dot(lo[...], member)
        return carry

    mid, last = cy // 2 + 1, cy - 1
    lon = [[lon_copies(which, group) for group in range(2)] for which in range(2)]
    lat = [lat_copies(0, field0), lat_copies(1, field1)]

    sweep(fill, 0, 0, 1, mid)
    pl.semaphore_wait(barrier, n_tile + n_band - 2)
    start_both(lon[0][0], tile, n_tile)
    sweep(fill, 0, 1, 0, 2, last)
    start_both(lat[0], band, n_band)
    sweep(fill, 0, 1, mid, last)
    start_both(lon[0][1], tile, n_tile)
    for load in smalls:
        load.wait()

    recv_lon(0, 0)
    sweep(first(0), 1, 0, 1, mid)
    start_both(lon[1][0], tile, n_tile)
    recv_lon(0, 1)
    recv_both(lat[0], band, n_band)
    sweep(first(1), 1, 1, 0, 2, last)
    start_both(lat[1], band, n_band)
    sweep(first(1), 1, 1, mid, last)
    start_both(lon[1][1], tile, n_tile)

    load_forcing.wait()
    recv_lon(1, 0)
    lax.fori_loop(1, mid, functools.partial(second, 0), 0)
    recv_lon(1, 1)
    lax.fori_loop(mid, last, functools.partial(second, 1), 0)
    recv_both(lat[1], band, n_band)
    lax.fori_loop(0, 2, lambda i, carry: second(1, i * last, carry), 0)
    store = pltpu.make_async_copy(work, res_ref, out_sem)
    store.start()

    nulls = [null_ref[0], null_ref[1]]
    parts = [RESTRICT_SCALE * coarse[f * nz : (f + 1) * nz, 0:cb] for f in range(nf)]
    products = [nulls[0] * nulls[0], nulls[0] * nulls[1], nulls[1] * nulls[1]]
    for k in range(2):
        products += [nulls[k] * part for part in parts]
    wide = lax.broadcasted_iota(jnp.int32, (nz, cx), 1)
    table = jnp.zeros((nz, cx), F32)
    for j, product in enumerate(products):
        table = jnp.where(wide == j, jnp.sum(product, axis=1, keepdims=True), table)
    square = jnp.concatenate([table, jnp.zeros((cx - nz, cx), F32)], axis=0)
    mom[tile] = jnp.transpose(square)[0:16, :]

    def mom_copy(partner, slot):
        return pltpu.make_async_remote_copy(
            src_ref=mom.at[tile], dst_ref=mom.at[slot],
            send_sem=mom_send.at[partner], recv_sem=mom_recv.at[slot],
            device_id=(band, partner), device_id_type=MESH,
        )

    for d in range(1, n_tile):
        mom_copy(lax.rem(tile + d, n_tile), tile).start()

    op = op_ref[...]
    ncol = op.shape[0]
    same = lax.broadcasted_iota(jnp.int32, (ncol, ncol), 0) == lax.broadcasted_iota(
        jnp.int32, (ncol, ncol), 1
    )
    diagonal = jnp.sum(jnp.where(same, op, 0.0), axis=0, keepdims=True)

    for d in range(1, n_tile):
        other = lax.rem(tile + d, n_tile)
        mom_copy(other, other).wait_recv()
    total = mom[0]
    for t in range(1, n_tile):
        total = total + mom[t]
    row = lambda j: total[j : j + 1, :]
    g00, g01, g11 = row(0), row(1), row(2)
    p0, p1 = total[3 : 3 + nf, :], total[3 + nf : 3 + 2 * nf, :]
    real = lax.broadcasted_iota(jnp.int32, (1, cx), 1) < nz
    det = jnp.where(real, g00 * g11 - g01 * g01, 1.0)
    c0 = (g11 * p0 - g01 * p1) / det
    c1 = (g00 * p1 - g01 * p0) / det
    coefs = jnp.concatenate([c0, c1, jnp.zeros((cx - 2 * nf, cx), F32)], axis=0)
    coefs = jnp.transpose(coefs)[0:nz, :]
    half = nf // 2
    deflated = [
        parts[f] - coefs[:, f : f + 1] * nulls[0] - coefs[:, nf + f : nf + f + 1] * nulls[1]
        for f in range(nf)
    ]
    slab = nz // n_band
    for f in range(half):
        both = jnp.concatenate([deflated[f], deflated[f + half]], axis=1)
        for d in range(n_band):
            slab_out[d, f * slab : (f + 1) * slab, :] = both[d * slab : (d + 1) * slab, :]

    def band_copy(out, into, sends, recvs, partner, slot):
        return pltpu.make_async_remote_copy(
            src_ref=out.at[partner], dst_ref=into.at[slot],
            send_sem=sends.at[partner], recv_sem=recvs.at[slot],
            device_id=(partner, tile), device_id_type=MESH,
        )

    def swap(out, into, sends, recvs):
        for d in range(1, n_band):
            band_copy(out, into, sends, recvs, lax.rem(band + d, n_band), band).start()
        into[band] = out[band]
        for d in range(1, n_band):
            other = lax.rem(band + d, n_band)
            band_copy(out, into, sends, recvs, other, other).wait_recv()

    swap(slab_out, slab_in, slab_send, slab_recv)
    pieces = [slab_in[b] for b in range(n_band)]
    lows = jnp.concatenate([piece[:, 0:cb] for piece in pieces], axis=1)
    highs = jnp.concatenate([piece[:, cb : 2 * cb] for piece in pieces], axis=1)
    columns = jnp.concatenate([lows, highs], axis=0)
    iterate = columns / diagonal
    for _ in range(SWEEPS - 1):
        applied = nt_dot(iterate, op, lax.Precision.HIGHEST)
        iterate = iterate + (columns - applied) / diagonal
    rows_half = half * slab
    for b in range(n_band):
        mine = slice(b * cb, (b + 1) * cb)
        back_out[b] = jnp.concatenate(
            [iterate[0:rows_half, mine], iterate[rows_half : 2 * rows_half, mine]], axis=1
        )
    swap(back_out, back_in, back_send, back_recv)
    inside = lax.broadcasted_iota(jnp.int32, (slab, 2 * cb), 1) < cb
    for d in range(n_band):
        for f in range(half):
            both = back_in[d, f * slab : (f + 1) * slab, :]
            z = slice(d * slab, (d + 1) * slab)
            smooth_ref[f, z, :] = jnp.where(inside, both, 0.0)
            smooth_ref[f + half, z, :] = jnp.where(inside, pltpu.roll(both, cb, 1), 0.0)

    for which in range(2):
        sent_both(lat[which], band, n_band)
        for group in range(2):
            sent_both(lon[which][group], tile, n_tile)
    for d in range(1, n_tile):
        mom_copy(lax.rem(tile + d, n_tile), tile).wait_send()
    for d in range(1, n_band):
        other = lax.rem(band + d, n_band)
        band_copy(slab_out, slab_in, slab_send, slab_recv, other, band).wait_send()
        band_copy(back_out, back_in, back_send, back_recv, other, band).wait_send()
    store.wait()


def finish_kernel(cy, ocean_ref, res_ref, smooth_ref, agg_ref, new_ref, out_ref):
    nz, cx = smooth_ref.shape[1:]
    value = smooth_ref[0]
    high = value.astype(BF16)
    low = (value - high.astype(F32)).astype(BF16)
    block = lax.broadcasted_iota(jnp.int32, (cx, cx), 0)
    for y in range(cy):
        member = jnp.where(block == agg_ref[y : y + 1, :], 1.0, 0.0).astype(BF16)
        add = jnp.dot(high, member, preferred_element_type=F32) + jnp.dot(
            low, member, preferred_element_type=F32
        )
        spot = pl.ds(y, nz, stride=cy)
        new_ref[0, spot, :] = ocean_ref[0, spot, :] + add
    out_ref[...] = res_ref[...]


def shards(
    n_band, n_tile, ocean_state, forcing, diffusivity, land_sea, aggregate, mixing, null_fields,
    coarse_op,
):
    nf, nz, cy, cx = ocean_state.shape
    cb = null_fields.shape[2]
    slab = nz // n_band
    ocean_rows = ocean_state.reshape(nf, nz * cy, cx)
    forcing_rows = forcing.reshape(nf, nz * cy, cx)
    dims = (n_band, n_tile, nf, nz, cy, cx, cb)
    any_spec = pl.BlockSpec(memory_space=pl.ANY)
    vmem = pl.BlockSpec(memory_space=pltpu.VMEM)
    field = pltpu.VMEM((nf, cy + 2, nz + 2 * PAD, cx), F32)
    strip = pltpu.VMEM((2, 2, nz, cx), F32)
    slabs = pltpu.VMEM((n_band, nf // 2 * slab, 2 * cb), F32)
    dma = pltpu.SemaphoreType.DMA
    cells = nf * nz * cy * cx
    residual, smoothed = pl.pallas_call(
        functools.partial(main_kernel, dims),
        out_shape=(
            jax.ShapeDtypeStruct((nf, nz * cy, cx), F32),
            jax.ShapeDtypeStruct((nf, nz, 2 * cb), F32),
        ),
        in_specs=[any_spec] * 8,
        out_specs=(any_spec, vmem),
        scratch_shapes=[
            pltpu.VMEM(diffusivity.shape, F32),
            pltpu.VMEM(land_sea.shape, land_sea.dtype),
            pltpu.VMEM(aggregate.shape, aggregate.dtype),
            pltpu.SMEM(mixing.shape, F32),
            pltpu.VMEM(null_fields.shape, F32),
            pltpu.VMEM(coarse_op.shape, F32),
            dma((6,)),
            pltpu.VMEM((nf, nz * cy, cx), F32),
            pltpu.VMEM((nf, nz * cy, cx), F32),
            field, field, strip, strip, strip, strip,
            pltpu.VMEM((nf * nz, cx), BF16),
            pltpu.VMEM((nf * nz, cx), BF16),
            pltpu.VMEM((nf * nz, cx), F32),
            pltpu.VMEM((n_tile, 16, cx), F32),
            slabs, slabs, slabs, slabs,
            dma((nf,)), dma, dma,
            dma((2, 2)), dma((2, 2)), dma((2, 2, 2)), dma((2, 2, 2)),
            dma((n_tile,)), dma((n_tile,)),
            dma((n_band,)), dma((n_band,)), dma((n_band,)), dma((n_band,)),
        ],
        compiler_params=pltpu.CompilerParams(
            collective_id=0, has_side_effects=True, vmem_limit_bytes=60 * MIB
        ),
        cost_estimate=pl.CostEstimate(
            flops=60 * cells, bytes_accessed=12 * cells, transcendentals=0
        ),
    )(ocean_rows, forcing_rows, diffusivity, land_sea, aggregate, mixing, null_fields, coarse_op)

    rows_spec = pl.BlockSpec((1, nz * cy, cx), lambda f: (f, 0, 0))
    new_state, residual = pl.pallas_call(
        functools.partial(finish_kernel, cy),
        grid=(nf,),
        out_shape=(
            jax.ShapeDtypeStruct((nf, nz * cy, cx), F32),
            jax.ShapeDtypeStruct((nf, nz * cy, cx), F32),
        ),
        in_specs=[
            rows_spec, rows_spec,
            pl.BlockSpec((1, nz, 2 * cb), lambda f: (f, 0, 0)),
            pl.BlockSpec((cy, cx), lambda f: (0, 0)),
        ],
        out_specs=(rows_spec, rows_spec),
        compiler_params=pltpu.CompilerParams(vmem_limit_bytes=24 * MIB),
        cost_estimate=pl.CostEstimate(
            flops=4 * cells, bytes_accessed=16 * cells, transcendentals=0
        ),
    )(ocean_rows, residual, smoothed, aggregate)
    shape = ocean_state.shape
    return (new_state.reshape(shape), residual.reshape(shape))


def solution(mesh):
    sizes = dict(mesh.shape)
    return jax.shard_map(
        functools.partial(shards, sizes["band"], sizes["tile"]),
        mesh=mesh,
        in_specs=(
            P(None, None, "band", "tile"),
            P(None, None, "band", "tile"),
            P("band", "tile"),
            P("band", "tile"),
            P("band", "tile"),
            P(),
            P(None, None, ("band", "tile")),
            P("tile", None),
        ),
        out_specs=(P(None, None, "band", "tile"), P(None, None, "band", "tile")),
        check_vma=False,
    )
```
